128 devices in a mesh: replica: 2 (over core), dp: 8 (over y, x_hi), tensor: 8 (over z, x_lo).
Axes of the slice: x: 4 (x_hi: 2, x_lo: 2; x = x_hi * 2 + x_lo), y: 4, z: 4, core: 2. Of those that a mesh axis runs over, the one named last changes fastest.
Arguments:
- tokens: bfloat16 [2, 1024, 4096], P('replica', 'tensor', 'dp'), may hold values from -6 to 6
- cotangent: bfloat16 [2, 1024, 4096], P('replica', 'tensor', 'dp'), may hold values from -0.75 to 0.75
- gate_weight: bfloat16 [2, 4096, 14336], P('replica', 'dp', 'tensor'), may hold values from -0.09375 to 0.09375
- up_weight: bfloat16 [2, 4096, 14336], P('replica', 'dp', 'tensor'), may hold values from -0.09375 to 0.09375
- down_weight: bfloat16 [2, 14336, 4096], P('replica', 'tensor', 'dp'), may hold values from -0.046875 to 0.046875
- frag_delta: bfloat16 [2, 14336, 4096], P('replica', 'tensor', 'dp'), may hold values from -6 to 6
- outer_momentum: float32 [14336, 4096], P('tensor', 'dp'), may hold values from -6 to 6
Outputs:
- mixed: bfloat16 [2, 1024, 4096], P('replica', 'tensor', 'dp')
- input_grad: bfloat16 [2, 1024, 4096], P('replica', 'tensor', 'dp')
- gate_weight_grad: bfloat16 [2, 4096, 14336], P('replica', 'dp', 'tensor')
- up_weight_grad: bfloat16 [2, 4096, 14336], P('replica', 'dp', 'tensor')
- down_weight_grad: bfloat16 [2, 14336, 4096], P('replica', 'tensor', 'dp')
- outer_step: float32 [14336, 4096], P('tensor', 'dp')
- momentum_next: float32 [14336, 4096], P('tensor', 'dp')
The draws below stay inside these ranges and needn't reach their ends.
All inputs are finite; a program needn't handle non-finite values.
Results may differ from the reference program's by a relative error of at most 0.033.
Values may be sent and summed in bfloat16 or wider, within the bound.
A program may use at most 128 MiB of HBM per device.

```python
import jax
import jax.numpy as jnp
from jax import lax

D = 4096
FF = 14336
TOKENS = 1024
N_REPLICA = 2
N_DP = 8
N_TENSOR = 8


def level_of(stream_key, shape, split, low, top_value):
    factor_of, own = 1.0, jax.random.fold_in(stream_key, 6)
    for position, shards_of in split:
        heights = jnp.exp(jax.random.uniform(jax.random.fold_in(own, position), (shards_of,), jnp.float32, low / len(split), top_value / len(split)))
        factor_of = factor_of * jnp.repeat(heights, shape[position] // shards_of).reshape([-1 if axis == position else 1 for axis in range(len(shape))])
    return factor_of


def bell_draw(rng, shape, scale, limit, shards=(), kind=jnp.bfloat16):
    result = scale * jax.random.normal(rng, shape, jnp.float32)
    if shards:
        result = result * level_of(rng, shape, shards, -0.22, 0.18)
    return jnp.clip(result, -limit, limit).astype(kind)


def setup_inputs(seed: int = 0) -> dict:
    arg_keys = jax.random.split(jax.random.key(seed), 8)
    tokens = bell_draw(arg_keys[0], (N_REPLICA, TOKENS, D), 1.0, 6.0, ((0, 2), (1, 8), (2, 8)))
    cotangent = bell_draw(arg_keys[1], (N_REPLICA, TOKENS, D), 0.125, 0.75, ((0, 2), (1, 8), (2, 8)))
    gate_weight = bell_draw(arg_keys[2], (N_REPLICA, D, FF), D ** -0.5, 0.09375, ((0, 2), (1, 8), (2, 8)))
    up_weight = bell_draw(arg_keys[3], (N_REPLICA, D, FF), D ** -0.5, 0.09375, ((0, 2), (1, 8), (2, 8)))
    down_weight = bell_draw(arg_keys[4], (N_REPLICA, FF, D), FF ** -0.5, 0.046875, ((0, 2), (1, 8), (2, 8)))
    frag_delta = bell_draw(arg_keys[5], (N_REPLICA, FF, D), 1.0, 6.0, ((0, 2), (1, 8), (2, 8)))
    outer_momentum = bell_draw(arg_keys[6], (FF, D), 1.0, 6.0, ((0, 8), (1, 8)), jnp.float32)
    return dict(tokens=tokens, cotangent=cotangent, gate_weight=gate_weight, up_weight=up_weight, down_weight=down_weight, frag_delta=frag_delta, outer_momentum=outer_momentum)


momentum_rate = 0.9
outer_rate = 0.7


def rounded(value):
    return lax.optimization_barrier(value.astype(jnp.bfloat16)).astype(jnp.float32)


def island(tokens, cotangent, gate_weight, up_weight, down_weight):
    width = D // N_DP
    hidden_width = FF // N_TENSOR
    gate = jnp.zeros((TOKENS, FF), jnp.float32)
    up = jnp.zeros((TOKENS, FF), jnp.float32)
    for block in range(N_DP):
        cols = slice(block * width, (block + 1) * width)
        gate = gate + rounded(jnp.dot(tokens[:, cols], gate_weight[cols], preferred_element_type=jnp.float32))
        up = up + rounded(jnp.dot(tokens[:, cols], up_weight[cols], preferred_element_type=jnp.float32))
    sigma = jax.nn.sigmoid(gate)
    active = gate * sigma
    hidden = (active * up).astype(jnp.bfloat16)
    mixed = jnp.zeros((TOKENS, D), jnp.float32)
    for block in range(N_TENSOR):
        units = slice(block * hidden_width, (block + 1) * hidden_width)
        mixed = mixed + rounded(jnp.dot(hidden[:, units], down_weight[units], preferred_element_type=jnp.float32))
    down_grad = jnp.dot(hidden.T, cotangent, preferred_element_type=jnp.float32).astype(jnp.bfloat16)
    hidden_grad = jnp.zeros((TOKENS, FF), jnp.float32)
    for block in range(N_DP):
        cols = slice(block * width, (block + 1) * width)
        hidden_grad = hidden_grad + rounded(jnp.dot(cotangent[:, cols], down_weight[:, cols].T, preferred_element_type=jnp.float32))
    gate_slope = (hidden_grad * up * sigma * (1.0 + gate * (1.0 - sigma))).astype(jnp.bfloat16)
    up_slope = (hidden_grad * active).astype(jnp.bfloat16)
    gate_grad = jnp.dot(tokens.T, gate_slope, preferred_element_type=jnp.float32).astype(jnp.bfloat16)
    up_grad = jnp.dot(tokens.T, up_slope, preferred_element_type=jnp.float32).astype(jnp.bfloat16)
    input_grad = jnp.zeros((TOKENS, D), jnp.float32)
    for block in range(N_TENSOR):
        units = slice(block * hidden_width, (block + 1) * hidden_width)
        term = jnp.dot(gate_slope[:, units], gate_weight[:, units].T, preferred_element_type=jnp.float32)
        term = term + jnp.dot(up_slope[:, units], up_weight[:, units].T, preferred_element_type=jnp.float32)
        input_grad = input_grad + rounded(term)
    return mixed.astype(jnp.bfloat16), input_grad.astype(jnp.bfloat16), gate_grad, up_grad, down_grad


def reference(tokens, cotangent, gate_weight, up_weight, down_weight, frag_delta, outer_momentum):
    results = [island(tokens[r], cotangent[r], gate_weight[r], up_weight[r], down_weight[r]) for r in range(N_REPLICA)]
    stacked = [jnp.stack([res[k] for res in results]) for k in range(5)]
    total = jnp.zeros((FF, D), jnp.float32)
    for r in range(N_REPLICA):
        total = total + frag_delta[r].astype(jnp.float32)
    mean_delta = total / N_REPLICA
    momentum_next = momentum_rate * outer_momentum + mean_delta
    outer_step = outer_rate * (mean_delta + momentum_rate * momentum_next)
    return (stacked[0], stacked[1], stacked[2], stacked[3], stacked[4], outer_step, momentum_next)
```

```python
import functools

import jax
import jax.numpy as jnp
from jax import lax
from jax.experimental import pallas as pl
from jax.experimental.pallas import tpu as pltpu
from jax.sharding import PartitionSpec as P

MESH = pl.DeviceIdType.MESH
F32 = jnp.float32
BF16 = jnp.bfloat16
momentum_rate = 0.9
outer_rate = 0.7

ROWS = 1024
OWN = 128
DIM = 512
UNITS = 1792
CHUNKS = 4
TC = ROWS // CHUNKS
SLOTS = 2
CY = 1024
CX = UNITS - CY
HY = CY // 2
HX = CX // 2
YB = TC // 4
XR = TC // 2
XB = XR // 4
TILE = 256
Z_ORDER = (0, 3, 1, 2)
SEMS = 160


def tick_order():
    order = []
    for tick in range(CHUNKS + 6):
        for stage, lag in (
            ("F", 5), ("E", 4), ("D", 3), ("C", 2), ("By", 1), ("A", 0), ("Bx", 1), ("G", 6),
        ):
            chunk = tick - lag
            if 0 <= chunk < CHUNKS:
                order += [(part, chunk) for part in PARTS[stage]]
    return order


PARTS = {
    "A": ("A",),
    "By": ("By",),
    "Bx": ("Bx",),
    "C": ("Cy", "Cx"),
    "D": ("Dy", "Dx"),
    "E": ("Ey", "Ex"),
    "F": ("Fy", "Fx"),
    "G": ("G",),
}


def pointwise(gate, up, hidden_grad):
    sigma = jax.nn.sigmoid(gate)
    active = gate * sigma
    hidden = active * up
    gate_slope = hidden_grad * up * sigma * (1.0 + gate * (1.0 - sigma))
    up_slope = hidden_grad * active
    return hidden.astype(BF16), gate_slope.astype(BF16), up_slope.astype(BF16)


def dot(a, b, ca=1, cb=0):
    return lax.dot_general(a, b, (((ca,), (cb,)), ((), ())), preferred_element_type=F32)


def kernel(
    tok_in, cot_in, wg_hbm, wu_hbm, wd_hbm, frag_in,
    mixed_out, ig_out, gg_out, ug_out, dg_out, frag_out,
    wg, wu, wd, tc_all, tc_t, part, h_all, ra, rb, sy, rc, e_own, xa, xb, xc, g_all, ms, rz, rx, gg, ug, dg,
    send_sem, recv_sem, local_sem,
):
    rep, d, t = lax.axis_index("replica"), lax.axis_index("dp"), lax.axis_index("tensor")
    y, xh = lax.div(d, 2), lax.rem(d, 2)
    z, xl = lax.div(t, 2), lax.rem(t, 2)
    x = 2 * xh + xl

    def at(yy, zz, xx):
        return (rep, yy * 2 + lax.div(xx, 2), zz * 2 + lax.rem(xx, 2))

    yp, ym, yo = lax.rem(y + 1, 4), lax.rem(y + 3, 4), lax.rem(y + 2, 4)
    xp, xm = lax.rem(x + 1, 4), lax.rem(x + 3, 4)
    zp, zm, zo = lax.rem(z + 1, 4), lax.rem(z + 3, 4), lax.rem(z + 2, 4)
    hp, hm = lax.div(xp, 2), lax.div(xm, 2)
    to_yp, to_ym = at(yp, z, x), at(ym, z, x)
    to_xp, to_xm = at(y, z, xp), at(y, z, xm)
    to_zp, to_zm, to_zo = at(y, zp, x), at(y, zm, x), at(y, zo, x)
    to_xl = (rep, d, 2 * z + 1 - xl)
    to_core = (1 - rep, d, t)

    count = [0]

    def remote(src, dst, target):
        k = count[0]
        count[0] += 1
        copy = pltpu.make_async_remote_copy(
            src_ref=src, dst_ref=dst, send_sem=send_sem.at[k], recv_sem=recv_sem.at[k],
            device_id=target, device_id_type=MESH,
        )
        copy.start()
        copies.append(copy)
        return copy

    copies = []
    sent = set()

    def wait_sent(copy):
        if id(copy) not in sent:
            sent.add(id(copy))
            copy.wait_send()

    loads = []
    for k, (src, dst) in enumerate(((wg_hbm, wg), (wu_hbm, wu), (wd_hbm, wd))):
        load = pltpu.make_async_copy(src, dst, local_sem.at[k])
        load.start()
        loads.append(load)

    def rows_of(start, size, step=16):
        return pl.ds(pl.multiple_of(start, step), size)

    own_rows = rows_of(t * OWN, OWN, OWN)
    mate_rows = rows_of((2 * z + 1 - xl) * OWN, OWN, OWN)
    tc_all[0, own_rows, :] = tok_in[...]
    tc_all[1, own_rows, :] = cot_in[...]

    barrier = pltpu.get_barrier_semaphore()
    peers = (to_yp, to_ym, to_xp, to_xm, to_zp, to_zm, to_zo, to_core)
    for peer in peers:
        pl.semaphore_signal(barrier, inc=1, device_id=peer, device_id_type=MESH)
    pl.semaphore_wait(barrier, len(peers))

    mate = remote(tc_all.at[:, own_rows], tc_all.at[:, own_rows], to_xl)
    gathers = [[], [], []]
    for k, target in enumerate((to_zp, to_zm, to_zo)):
        gathers[k].append(remote(tc_all.at[:, own_rows], tc_all.at[:, own_rows], target))
    frag_copy = remote(frag_in, frag_out, to_core)
    for load in loads:
        load.wait()

    live = [dict() for _ in range(CHUNKS)]

    def row0(c):
        return lax.rem(z + Z_ORDER[c], 4) * TC

    def stage_a(c):
        s, r0, me = c % SLOTS, row0(c), live[c]
        if c == 0:
            mate.wait_recv()
            for k, target in enumerate((to_zp, to_zm, to_zo)):
                gathers[k].append(remote(tc_all.at[:, mate_rows], tc_all.at[:, mate_rows], target))
        else:
            for copy in gathers[c - 1]:
                copy.wait_recv()
        if c >= SLOTS:
            for copy in live[c - SLOTS]["part_sends"]:
                wait_sent(copy)
        rows = rows_of(r0, TC, TC)

        def tile(k, carry):
            cols = pl.ds(pl.multiple_of(k * TILE, TILE), TILE)
            tok, cot = tc_all[0, rows, :], tc_all[1, rows, :]
            part[s, 0, :, cols] = dot(tok, wg[:, cols]).astype(BF16)
            part[s, 1, :, cols] = dot(tok, wu[:, cols]).astype(BF16)
            part[s, 2, :, cols] = dot(cot, wd[cols, :], 1, 1).astype(BF16)
            return carry

        lax.fori_loop(0, CY // TILE, tile, 0)
        ps = part.at[s]
        opp, up_b, down_b = rows_of(yo * YB, YB), rows_of(yp * YB, YB), rows_of(ym * YB, YB)
        me["s1"] = [
            remote(ps.at[:, opp, pl.ds(0, HY)], ra.at[c, 0], to_yp),
            remote(ps.at[:, opp, pl.ds(HY, HY)], ra.at[c, 1], to_ym),
            remote(ps.at[:, up_b, pl.ds(HY, HY)], rb.at[c, 0, :, :, pl.ds(HY, HY)], to_yp),
            remote(ps.at[:, down_b, pl.ds(0, HY)], rb.at[c, 1, :, :, pl.ds(0, HY)], to_ym),
        ]
        lax.fori_loop(CY // TILE, UNITS // TILE, tile, 0)
        me["t1"] = [
            remote(ps.at[:, rows_of(hp * XR, XR), pl.ds(CY, CX)], xa.at[c, 0], to_xp),
            remote(ps.at[:, rows_of(hm * XR, XR), pl.ds(CY, CX)], xa.at[c, 1], to_xm),
        ]
        me["part_sends"] = me["s1"] + me["t1"]
        for k in range(2):
            tc_t[k, :, rows] = tc_all[k, rows, :].T

    def stage_by(c):
        s, me = c % SLOTS, live[c]
        ps = part.at[s]
        me["s2"] = []
        for k, (blk, target) in enumerate(((yp, to_yp), (ym, to_ym))):
            rows, cols = rows_of(blk * YB, YB), pl.ds(k * HY, HY)
            me["s1"][k].wait_recv()
            for a in range(3):
                part[s, a, rows, cols] = (part[s, a, rows, cols].astype(F32) + ra[c, k, a].astype(F32)).astype(BF16)
            me["s2"].append(remote(ps.at[:, rows, cols], rb.at[c, k, :, :, cols], target))
        me["part_sends"] += me["s2"]

    def stage_bx(c):
        me = live[c]
        for copy in me["t1"]:
            copy.wait_recv()
        for blk in (yo, yp, ym):
            rows = rows_of(blk * XB, XB)
            for a in range(3):
                xa[c, 0, a, rows, :] = (xa[c, 0, a, rows, :].astype(F32) + xa[c, 1, a, rows, :].astype(F32)).astype(BF16)
            if blk is yo:
                me["t2"] = [
                    remote(xa.at[c, 0, :, rows, pl.ds(0, HX)], xb.at[c, 0], to_yp),
                    remote(xa.at[c, 0, :, rows, pl.ds(HX, HX)], xb.at[c, 1], to_ym),
                ]
        me["t3"] = [
            remote(xa.at[c, 0, :, rows_of(yp * XB, XB), pl.ds(HX, HX)], xc.at[c, 0, :, :, pl.ds(HX, HX)], to_yp),
            remote(xa.at[c, 0, :, rows_of(ym * XB, XB), pl.ds(0, HX)], xc.at[c, 1, :, :, pl.ds(0, HX)], to_ym),
        ]

    def stage_cy(c):
        s, me = c % SLOTS, live[c]
        for copy in me["s1"][2:] + me["s2"]:
            copy.wait_recv()
        rows = rows_of(y * YB, YB)
        for h in range(2):
            cols = pl.ds(h * HY, HY)
            for a in range(3):
                total = part[s, a, rows, cols].astype(F32) + rb[c, 0, a, :, cols].astype(F32)
                sy[c, h, a] = (total + rb[c, 1, a, :, cols].astype(F32)).astype(BF16)
        me["s3"] = [
            remote(sy.at[c, hp], rc.at[c, 0], to_xp),
            remote(sy.at[c, hm], rc.at[c, 1], to_xm),
        ]

    def stage_cx(c):
        me = live[c]
        for k, (blk, target) in enumerate(((yp, to_yp), (ym, to_ym))):
            rows, cols = rows_of(blk * XB, XB), pl.ds(k * HX, HX)
            me["t2"][k].wait_recv()
            for a in range(3):
                xa[c, 0, a, rows, cols] = (xa[c, 0, a, rows, cols].astype(F32) + xb[c, k, a].astype(F32)).astype(BF16)
            me["t3"].append(remote(xa.at[c, 0, :, rows, cols], xc.at[c, k, :, :, cols], target))

    def stage_dy(c):
        me = live[c]
        for copy in me["s3"]:
            copy.wait_recv()
        sums = [rc[c, 0, a].astype(F32) + rc[c, 1, a].astype(F32) for a in range(3)]
        for a, value in enumerate(pointwise(*sums)):
            e_own[c, a] = value
        place = h_all.at[:, rows_of(row0(c) + y * YB, YB), pl.ds(pl.multiple_of(xh * HY, HY), HY)]
        me["s4"] = [remote(e_own.at[c], place, target) for target in (to_xp, to_xm)]

    def stage_dx(c):
        me = live[c]
        for copy in me["t3"]:
            copy.wait_recv()
        rows = rows_of(y * XB, XB)
        sums = []
        for a in range(3):
            total = xa[c, 0, a, rows, :].astype(F32) + xa[c, 1, a, rows, :].astype(F32)
            sums.append(total + (xc[c, 0, a].astype(F32) + xc[c, 1, a].astype(F32)))
        for a, value in enumerate(pointwise(*sums)):
            g_all[c, a, rows, :] = value
        place = g_all.at[c, :, rows]
        me["t4"] = [remote(place, place, target) for target in (to_yp, to_ym)]

    def stage_ey(c):
        me = live[c]
        for copy in me["s4"]:
            copy.wait_recv()
        place = h_all.at[:, rows_of(row0(c) + y * YB, YB), pl.ds(0, CY)]
        me["s5"] = [remote(place, place, target) for target in (to_yp, to_ym)]

    def stage_ex(c):
        me = live[c]
        me["t5"] = []
        for k, (blk, target) in enumerate(((ym, to_yp), (yp, to_ym))):
            me["t4"][k].wait_recv()
            place = g_all.at[c, :, rows_of(blk * XB, XB), pl.ds(k * HX, HX)]
            me["t5"].append(remote(place, place, target))

    def stage_fy(c):
        me = live[c]
        me["s6"] = []
        for k, (blk, target) in enumerate(((ym, to_yp), (yp, to_ym))):
            me["s5"][k].wait_recv()
            place = h_all.at[:, rows_of(row0(c) + blk * YB, YB), pl.ds(k * HY, HY)]
            me["s6"].append(remote(place, place, target))

    def stage_fx(c):
        me = live[c]
        for copy in me["t5"]:
            copy.wait_recv()
        place = h_all.at[:, rows_of(row0(c) + xh * XR, XR), pl.ds(CY, CX)]
        me["t6"] = [remote(g_all.at[c], place, target) for target in (to_xp, to_xm)]

    zsum = []

    def stage_g(c):
        me = live[c]
        for copy in me["s6"] + me["t6"]:
            copy.wait_recv()
        rows = rows_of(row0(c), TC, TC)

        def tile(k, carry):
            cols = pl.ds(pl.multiple_of(k * TILE, TILE), TILE)
            ms[c, 0, :, cols] = dot(h_all[0, rows, :], wd[:, cols]).astype(BF16)
            term = dot(h_all[1, rows, :], wg[cols, :], 1, 1) + dot(h_all[2, rows, :], wu[cols, :], 1, 1)
            ms[c, 1, :, cols] = term.astype(BF16)
            return carry

        lax.fori_loop(0, DIM // TILE, tile, 0)
        if c:
            zsum.append(remote(ms.at[c], rz.at[c - 1], (to_zm, to_zp, to_zo)[c - 1]))

    stages = dict(
        A=stage_a, By=stage_by, Bx=stage_bx, Cy=stage_cy, Cx=stage_cx, Dy=stage_dy, Dx=stage_dx,
        Ey=stage_ey, Ex=stage_ex, Fy=stage_fy, Fx=stage_fx, G=stage_g,
    )
    for name, c in tick_order():
        stages[name](c)

    def grad_tile(k, carry):
        cols = pl.ds(pl.multiple_of(k * TILE, TILE), TILE)
        gg[:, cols] = dot(tc_t[0], h_all[1, :, cols]).astype(BF16)
        ug[:, cols] = dot(tc_t[0], h_all[2, :, cols]).astype(BF16)
        dg[cols, :] = dot(tc_t[1], h_all[0, :, cols]).astype(BF16).T
        return carry

    lax.fori_loop(0, UNITS // TILE, grad_tile, 0)
    stores = []
    for k, (src, dst) in enumerate(((gg, gg_out), (ug, ug_out), (dg, dg_out))):
        store = pltpu.make_async_copy(src, dst, local_sem.at[3 + k])
        store.start()
        stores.append(store)

    for copy in zsum:
        copy.wait_recv()
    mine, theirs = rows_of(xl * OWN, OWN, OWN), rows_of((1 - xl) * OWN, OWN, OWN)

    def zsum_of(k, rows):
        total = ms[0, k, rows, :].astype(F32)
        for j in range(3):
            total = total + rz[j, k, rows, :].astype(F32)
        return total

    for k in range(2):
        ms[0, k, theirs, :] = zsum_of(k, theirs).astype(BF16)
    last = remote(ms.at[0, :, theirs], rx, to_xl)
    totals = [zsum_of(k, mine) for k in range(2)]
    last.wait_recv()
    mixed_out[...] = (totals[0] + rx[0].astype(F32)).astype(BF16)
    ig_out[...] = (totals[1] + rx[1].astype(F32)).astype(BF16)
    frag_copy.wait_recv()
    for copy in copies:
        wait_sent(copy)
    for store in stores:
        store.wait()


def shards(tokens, cotangent, gate_weight, up_weight, down_weight, frag_delta, outer_momentum):
    vmem, anywhere = pl.BlockSpec(memory_space=pltpu.VMEM), pl.BlockSpec(memory_space=pl.ANY)
    side = jax.ShapeDtypeStruct((OWN, DIM), BF16)
    wide = jax.ShapeDtypeStruct((DIM, UNITS), BF16)
    tall = jax.ShapeDtypeStruct((UNITS, DIM), BF16)
    mixed, input_grad, gate_grad, up_grad, down_grad, other = pl.pallas_call(
        kernel,
        out_shape=(side, side, wide, wide, tall, tall),
        in_specs=[vmem, vmem] + [anywhere] * 4,
        out_specs=(vmem, vmem, anywhere, anywhere, anywhere, anywhere),
        scratch_shapes=[
            pltpu.VMEM((DIM, UNITS), BF16),
            pltpu.VMEM((DIM, UNITS), BF16),
            pltpu.VMEM((UNITS, DIM), BF16),
            pltpu.VMEM((2, ROWS, DIM), BF16),
            pltpu.VMEM((2, DIM, ROWS), BF16),
            pltpu.VMEM((SLOTS, 3, TC, UNITS), BF16),
            pltpu.VMEM((3, ROWS, UNITS), BF16),
            pltpu.VMEM((CHUNKS, 2, 3, YB, HY), BF16),
            pltpu.VMEM((CHUNKS, 2, 3, YB, CY), BF16),
            pltpu.VMEM((CHUNKS, 2, 3, YB, HY), BF16),
            pltpu.VMEM((CHUNKS, 2, 3, YB, HY), BF16),
            pltpu.VMEM((CHUNKS, 3, YB, HY), BF16),
            pltpu.VMEM((CHUNKS, 2, 3, XR, CX), BF16),
            pltpu.VMEM((CHUNKS, 2, 3, XB, HX), BF16),
            pltpu.VMEM((CHUNKS, 2, 3, XB, CX), BF16),
            pltpu.VMEM((CHUNKS, 3, XR, CX), BF16),
            pltpu.VMEM((CHUNKS, 2, TC, DIM), BF16),
            pltpu.VMEM((3, 2, TC, DIM), BF16),
            pltpu.VMEM((2, OWN, DIM), BF16),
            pltpu.VMEM((DIM, UNITS), BF16),
            pltpu.VMEM((DIM, UNITS), BF16),
            pltpu.VMEM((UNITS, DIM), BF16),
            pltpu.SemaphoreType.DMA((SEMS,)),
            pltpu.SemaphoreType.DMA((SEMS,)),
            pltpu.SemaphoreType.DMA((6,)),
        ],
        compiler_params=pltpu.CompilerParams(
            collective_id=0, has_side_effects=True, vmem_limit_bytes=60 * 1024 * 1024
        ),
        cost_estimate=pl.CostEstimate(flops=18 * ROWS * DIM * UNITS, bytes_accessed=16_000_000, transcendentals=0),
        name="layer",
    )(tokens[0], cotangent[0], gate_weight[0], up_weight[0], down_weight[0], frag_delta[0])
    mean_delta = (frag_delta[0].astype(F32) + other.astype(F32)) / lax.axis_size("replica")
    momentum_next = momentum_rate * outer_momentum + mean_delta
    outer_step = outer_rate * (mean_delta + momentum_rate * momentum_next)
    return (
        mixed[None], input_grad[None], gate_grad[None], up_grad[None], down_grad[None],
        outer_step, momentum_next,
    )


def solution(mesh):
    act, wide, tall = P("replica", "tensor", "dp"), P("replica", "dp", "tensor"), P("replica", "tensor", "dp")
    state = P("tensor", "dp")
    return jax.shard_map(
        shards,
        mesh=mesh,
        in_specs=(act, act, wide, wide, tall, tall, state),
        out_specs=(act, act, wide, wide, tall, state, state),
        check_vma=False,
    )
```

```python
import functools

import jax
import jax.numpy as jnp
from jax import lax
from jax.experimental import pallas as pl
from jax.experimental.pallas import tpu as pltpu
from jax.sharding import PartitionSpec as P

MESH = pl.DeviceIdType.MESH
F32 = jnp.float32
BF16 = jnp.bfloat16
momentum_rate = 0.9
outer_rate = 0.7

ROWS = 1024
OWN = 128
DIM = 512
UNITS = 1792
SIZES = (128, 256, 256, 256, 128)
STARTS = (0, 128, 384, 640, 896)
CHUNKS = len(SIZES)
SLOTS = 2
CY = 1024
CX = UNITS - CY
HY = CY // 2
HX = CX // 2
TILE = 256
SEMS = 224

ORDER = (
    "A0", "By0", "Bx0", "Bz0", "M0", "Cy0", "Cx0", "Dx0", "Dy0", "A1", "Ex0", "Ey0", "A2", "By1", "Bx1", "Fx0",
    "Bz1", "Fy0", "By2", "Bx2", "Cy1", "Bz2", "Cx1", "A3", "G0", "Dy1", "Cy2", "Cx2", "A4", "Bx3", "Dx1", "By3",
    "Bz3", "Dx2", "Ey1", "By4", "Cx3", "Dy2", "Bx4", "Ex1", "Bz4", "Cy3", "Ex2", "Ey2", "Fy1", "Cy4", "Dx3", "Cx4",
    "Fx1", "Dy3", "Fx2", "Dy4", "Fy2", "G1", "Ex3", "Dx4", "Ey3", "G2", "Fx3", "Ey4", "Ex4", "Fy3", "Fy4", "Fx4",
    "G3", "G4",
)


def pointwise(gate, up, hidden_grad):
    sigma = jax.nn.sigmoid(gate)
    active = gate * sigma
    hidden = active * up
    gate_slope = hidden_grad * up * sigma * (1.0 + gate * (1.0 - sigma))
    up_slope = hidden_grad * active
    return hidden.astype(BF16), gate_slope.astype(BF16), up_slope.astype(BF16)


def dot(a, b, ca=1, cb=0):
    return lax.dot_general(a, b, (((ca,), (cb,)), ((), ())), preferred_element_type=F32)


def kernel(
    tok_in, cot_in, wg_hbm, wu_hbm, wd_hbm, frag_in,
    mixed_out, ig_out, gg_out, ug_out, dg_out, frag_out,
    wg, wu, wd, tc_all, tc_t, part, h_all, ra, rb, sy, rc, e_own, xa, xb, xc, g_all, ms, ml, own, rz, rx, gg, ug, dg,
    send_sem, recv_sem, local_sem,
):
    rep, d, t = lax.axis_index("replica"), lax.axis_index("dp"), lax.axis_index("tensor")
    y, xh = lax.div(d, 2), lax.rem(d, 2)
    z, xl = lax.div(t, 2), lax.rem(t, 2)
    x = 2 * xh + xl

    def at(yy, zz, xx):
        return (rep, yy * 2 + lax.div(xx, 2), zz * 2 + lax.rem(xx, 2))

    yp, ym, yo = lax.rem(y + 1, 4), lax.rem(y + 3, 4), lax.rem(y + 2, 4)
    xp, xm = lax.rem(x + 1, 4), lax.rem(x + 3, 4)
    zp, zm, zo = lax.rem(z + 1, 4), lax.rem(z + 3, 4), lax.rem(z + 2, 4)
    hp, hm = lax.div(xp, 2), lax.div(xm, 2)
    to_yp, to_ym = at(yp, z, x), at(ym, z, x)
    to_xp, to_xm = at(y, z, xp), at(y, z, xm)
    to_zp, to_zm, to_zo = at(y, zp, x), at(y, zm, x), at(y, zo, x)
    to_xl = (rep, d, 2 * z + 1 - xl)
    to_core = (1 - rep, d, t)

    count = [0]

    def remote(src, dst, target):
        k = count[0]
        count[0] += 1
        copy = pltpu.make_async_remote_copy(
            src_ref=src, dst_ref=dst, send_sem=send_sem.at[k], recv_sem=recv_sem.at[k],
            device_id=target, device_id_type=MESH,
        )
        copy.start()
        copies.append(copy)
        return copy

    copies = []
    sent = set()

    def wait_sent(copy):
        if id(copy) not in sent:
            sent.add(id(copy))
            copy.wait_send()

    loads = []
    for k, (src, dst) in enumerate(((wg_hbm, wg), (wu_hbm, wu), (wd_hbm, wd))):
        load = pltpu.make_async_copy(src, dst, local_sem.at[k])
        load.start()
        loads.append(load)

    def rows_of(start, size, step=16):
        return pl.ds(pl.multiple_of(start, step), size)

    own_rows = rows_of(t * OWN, OWN, OWN)
    mate_rows = rows_of((2 * z + 1 - xl) * OWN, OWN, OWN)
    tc_all[0, own_rows, :] = tok_in[...]
    tc_all[1, own_rows, :] = cot_in[...]

    barrier = pltpu.get_barrier_semaphore()
    peers = (to_yp, to_ym, to_xp, to_xm, to_zp, to_zm, to_zo, to_core)
    for peer in peers:
        pl.semaphore_signal(barrier, inc=1, device_id=peer, device_id_type=MESH)
    pl.semaphore_wait(barrier, len(peers))

    mate = remote(tc_all.at[:, own_rows], tc_all.at[:, own_rows], to_xl)
    z_targets = (to_zp, to_zm, to_zo)
    gathers = [[remote(tc_all.at[:, own_rows], tc_all.at[:, own_rows], target)] for target in z_targets]
    frag_copy = remote(frag_in, frag_out, to_core)
    for load in loads:
        load.wait()

    live = [dict() for _ in range(CHUNKS)]

    def row0(c, side):
        if c in (1, 2, 3):
            return (zm, zp, zo)[c - 1] * 2 * OWN
        return (2 * z + (side if c == 0 else 1 - side)) * OWN

    def y_rows(c, blk, base=0):
        return rows_of(base + blk * (SIZES[c] // 4), SIZES[c] // 4)

    def x_rows(c, blk, base=0):
        return rows_of(base + blk * (SIZES[c] // 8), SIZES[c] // 8)

    def y_own(c):
        return pl.ds(STARTS[c] // 4, SIZES[c] // 4)

    def x_own(c):
        return pl.ds(STARTS[c] // 8, SIZES[c] // 8)

    def xa_rows(c, blk):
        return x_rows(c, blk, STARTS[c] // 2)

    def stage_m(c):
        mate.wait_recv()
        for k, target in enumerate(z_targets):
            gathers[k].append(remote(tc_all.at[:, mate_rows], tc_all.at[:, mate_rows], target))

    def stage_a(c):
        s, size, me = c % SLOTS, SIZES[c], live[c]
        if c in (1, 2, 3):
            for copy in gathers[c - 1]:
                copy.wait_recv()
        if c >= SLOTS:
            for copy in live[c - SLOTS]["part_sends"]:
                wait_sent(copy)
        rows = rows_of(row0(c, xl), size, OWN)
        kept = pl.ds(0, size)

        def tile(k, carry):
            cols = pl.ds(pl.multiple_of(k * TILE, TILE), TILE)
            tok, cot = tc_all[0, rows, :], tc_all[1, rows, :]
            part[s, 0, kept, cols] = dot(tok, wg[:, cols]).astype(BF16)
            part[s, 1, kept, cols] = dot(tok, wu[:, cols]).astype(BF16)
            part[s, 2, kept, cols] = dot(cot, wd[cols, :], 1, 1).astype(BF16)
            return carry

        lax.fori_loop(0, CY // TILE, tile, 0)
        ps = part.at[s]
        first, second = pl.ds(0, HY), pl.ds(HY, HY)
        me["s1"] = [
            remote(ps.at[:, y_rows(c, yo), first], ra.at[0, :, y_own(c)], to_yp),
            remote(ps.at[:, y_rows(c, yo), second], ra.at[1, :, y_own(c)], to_ym),
            remote(ps.at[:, y_rows(c, yp), second], rb.at[0, :, y_own(c), second], to_yp),
            remote(ps.at[:, y_rows(c, ym), first], rb.at[1, :, y_own(c), first], to_ym),
        ]
        lax.fori_loop(CY // TILE, UNITS // TILE, tile, 0)
        me["t1"] = []
        for blk in (yo, yp, ym, y):
            for k, (half, target) in enumerate(((hp, to_xp), (hm, to_xm))):
                src = ps.at[:, x_rows(c, blk, half * (size // 2)), pl.ds(CY, CX)]
                me["t1"].append(remote(src, xa.at[k, :, xa_rows(c, blk)], target))
        me["part_sends"] = me["s1"] + me["t1"]
        for k in range(2):
            tc_t[k, :, rows] = tc_all[k, rows, :].T

    def stage_by(c):
        s, me = c % SLOTS, live[c]
        me["s2"] = []
        for k, (blk, target) in enumerate(((yp, to_yp), (ym, to_ym))):
            rows, cols = y_rows(c, blk), pl.ds(k * HY, HY)
            me["s1"][k].wait_recv()
            for a in range(3):
                total = part[s, a, rows, cols].astype(F32) + ra[k, a, y_own(c), :].astype(F32)
                part[s, a, rows, cols] = total.astype(BF16)
            me["s2"].append(remote(part.at[s, :, rows, cols], rb.at[k, :, y_own(c), cols], target))
        me["part_sends"] += me["s2"]

    def add_sides(c, blk):
        rows = xa_rows(c, blk)
        for a in range(3):
            xa[0, a, rows, :] = (xa[0, a, rows, :].astype(F32) + xa[1, a, rows, :].astype(F32)).astype(BF16)

    def stage_bx(c):
        me = live[c]
        for copy in me["t1"][:2]:
            copy.wait_recv()
        add_sides(c, yo)
        rows = xa_rows(c, yo)
        me["t2"] = [
            remote(xa.at[0, :, rows, pl.ds(0, HX)], xb.at[0, :, x_own(c)], to_yp),
            remote(xa.at[0, :, rows, pl.ds(HX, HX)], xb.at[1, :, x_own(c)], to_ym),
        ]

    def stage_bz(c):
        me = live[c]
        for copy in me["t1"][2:6]:
            copy.wait_recv()
        me["t3"] = []
        for k, (blk, target) in enumerate(((yp, to_yp), (ym, to_ym))):
            add_sides(c, blk)
            cols = pl.ds((1 - k) * HX, HX)
            me["t3"].append(remote(xa.at[0, :, xa_rows(c, blk), cols], xc.at[k, :, x_own(c), cols], target))

    def stage_cy(c):
        s, me = c % SLOTS, live[c]
        for copy in me["s1"][2:] + me["s2"]:
            copy.wait_recv()
        rows, own = y_rows(c, y), y_own(c)
        for h in range(2):
            cols = pl.ds(h * HY, HY)
            for a in range(3):
                total = part[s, a, rows, cols].astype(F32) + rb[0, a, own, cols].astype(F32)
                sy[h, a, own, :] = (total + rb[1, a, own, cols].astype(F32)).astype(BF16)
        me["s3"] = [
            remote(sy.at[half, :, own], rc.at[k, :, own], target)
            for k, (half, target) in enumerate(((hp, to_xp), (hm, to_xm)))
        ]

    def stage_cx(c):
        me = live[c]
        for k, (blk, target) in enumerate(((yp, to_yp), (ym, to_ym))):
            rows, cols = xa_rows(c, blk), pl.ds(k * HX, HX)
            me["t2"][k].wait_recv()
            for a in range(3):
                total = xa[0, a, rows, cols].astype(F32) + xb[k, a, x_own(c), :].astype(F32)
                xa[0, a, rows, cols] = total.astype(BF16)
            me["t3"].append(remote(xa.at[0, :, rows, cols], xc.at[k, :, x_own(c), cols], target))

    def stage_dy(c):
        me, own = live[c], y_own(c)
        for copy in me["s3"]:
            copy.wait_recv()
        sums = [rc[0, a, own, :].astype(F32) + rc[1, a, own, :].astype(F32) for a in range(3)]
        for a, value in enumerate(pointwise(*sums)):
            e_own[a, own, :] = value
        place = h_all.at[:, y_rows(c, y, row0(c, 1 - xl)), pl.ds(pl.multiple_of(xh * HY, HY), HY)]
        me["s4"] = [remote(e_own.at[:, own], place, target) for target in (to_xp, to_xm)]

    def send_x(c, blk):
        place = h_all.at[:, x_rows(c, blk, row0(c, 1 - xl) + xh * (SIZES[c] // 2)), pl.ds(CY, CX)]
        live[c]["t6"] += [remote(g_all.at[:, xa_rows(c, blk)], place, target) for target in (to_xp, to_xm)]

    def stage_dx(c):
        me, own = live[c], x_own(c)
        for copy in me["t3"] + me["t1"][6:]:
            copy.wait_recv()
        rows = xa_rows(c, y)
        sums = []
        for a in range(3):
            total = xa[0, a, rows, :].astype(F32) + xa[1, a, rows, :].astype(F32)
            sums.append(total + (xc[0, a, own, :].astype(F32) + xc[1, a, own, :].astype(F32)))
        for a, value in enumerate(pointwise(*sums)):
            g_all[a, rows, :] = value
        place = g_all.at[:, rows]
        me["t4"] = [remote(place, place, target) for target in (to_yp, to_ym)]
        me["t6"] = []
        send_x(c, y)

    def stage_ey(c):
        me = live[c]
        for copy in me["s4"]:
            copy.wait_recv()
        place = h_all.at[:, y_rows(c, y, row0(c, xl)), pl.ds(0, CY)]
        me["s5"] = [remote(place, place, target) for target in (to_yp, to_ym)]

    def stage_ex(c):
        me = live[c]
        me["t5"] = []
        for k, (blk, target) in enumerate(((ym, to_yp), (yp, to_ym))):
            me["t4"][k].wait_recv()
            place = g_all.at[:, xa_rows(c, blk), pl.ds(k * HX, HX)]
            me["t5"].append(remote(place, place, target))
        for blk in (ym, yp):
            send_x(c, blk)

    def stage_fy(c):
        me = live[c]
        me["s6"] = []
        for k, (blk, target) in enumerate(((ym, to_yp), (yp, to_ym))):
            me["s5"][k].wait_recv()
            place = h_all.at[:, y_rows(c, blk, row0(c, xl)), pl.ds(k * HY, HY)]
            me["s6"].append(remote(place, place, target))

    def stage_fx(c):
        for copy in live[c]["t5"]:
            copy.wait_recv()
        send_x(c, yo)

    zsum = []
    last = []

    def stage_g(c):
        me = live[c]
        for copy in me["s6"] + me["t6"]:
            copy.wait_recv()
        rows = rows_of(row0(c, xl), SIZES[c], OWN)
        if c == 4:
            for copy in zsum:
                copy.wait_recv()

        def keep(k, cols, value):
            if c == 0:
                own[k, :, cols] = value
            elif c == 4:
                ml[k, :, cols] = (value + z_sum(k, 1 - xl, cols)).astype(BF16)
            else:
                ms[c - 1, k, :, cols] = value.astype(BF16)

        def mixed_tile(k, carry):
            cols = pl.ds(pl.multiple_of(k * TILE, TILE), TILE)
            keep(0, cols, dot(h_all[0, rows, :], wd[:, cols]))
            return carry

        def ig_tile(k, carry):
            cols = pl.ds(pl.multiple_of(k * TILE, TILE), TILE)
            term = dot(h_all[1, rows, :], wg[cols, :], 1, 1) + dot(h_all[2, rows, :], wu[cols, :], 1, 1)
            keep(1, cols, term)
            return carry

        for k, body in enumerate((mixed_tile, ig_tile)):
            lax.fori_loop(0, DIM // TILE, body, 0)
            if c == 4:
                last.append(remote(ml.at[k], rx.at[k], to_xl))
        if c in (1, 2, 3):
            zsum.append(remote(ms.at[c - 1], rz.at[c - 1], (to_zm, to_zp, to_zo)[c - 1]))

    def z_sum(k, side, cols):
        rows = rows_of(side * OWN, OWN, OWN)
        total = rz[0, k, rows, cols].astype(F32) + rz[1, k, rows, cols].astype(F32)
        return total + rz[2, k, rows, cols].astype(F32)

    stages = dict(
        A=stage_a, M=stage_m, By=stage_by, Bx=stage_bx, Bz=stage_bz, Cy=stage_cy, Cx=stage_cx, Dy=stage_dy,
        Dx=stage_dx, Ey=stage_ey, Ex=stage_ex, Fy=stage_fy, Fx=stage_fx, G=stage_g,
    )
    for step in ORDER:
        stages[step[:-1]](int(step[-1]))

    def grad_tile(k, carry):
        cols = pl.ds(pl.multiple_of(k * TILE, TILE), TILE)
        gg[:, cols] = dot(tc_t[0], h_all[1, :, cols]).astype(BF16)
        ug[:, cols] = dot(tc_t[0], h_all[2, :, cols]).astype(BF16)
        dg[cols, :] = dot(tc_t[1], h_all[0, :, cols]).astype(BF16).T
        return carry

    lax.fori_loop(0, UNITS // TILE, grad_tile, 0)
    stores = []
    for k, (src, dst) in enumerate(((gg, gg_out), (ug, ug_out), (dg, dg_out))):
        store = pltpu.make_async_copy(src, dst, local_sem.at[3 + k])
        store.start()
        stores.append(store)

    for k, out in enumerate((mixed_out, ig_out)):
        total = own[k] + z_sum(k, xl, pl.ds(0, DIM))
        last[k].wait_recv()
        out[...] = (total + rx[k].astype(F32)).astype(BF16)
    frag_copy.wait_recv()
    for copy in copies:
        wait_sent(copy)
    for store in stores:
        store.wait()


def shards(tokens, cotangent, gate_weight, up_weight, down_weight, frag_delta, outer_momentum):
    vmem, anywhere = pl.BlockSpec(memory_space=pltpu.VMEM), pl.BlockSpec(memory_space=pl.ANY)
    side = jax.ShapeDtypeStruct((OWN, DIM), BF16)
    wide = jax.ShapeDtypeStruct((DIM, UNITS), BF16)
    tall = jax.ShapeDtypeStruct((UNITS, DIM), BF16)
    mixed, input_grad, gate_grad, up_grad, down_grad, other = pl.pallas_call(
        kernel,
        out_shape=(side, side, wide, wide, tall, tall),
        in_specs=[vmem, vmem] + [anywhere] * 4,
        out_specs=(vmem, vmem, anywhere, anywhere, anywhere, anywhere),
        scratch_shapes=[
            pltpu.VMEM((DIM, UNITS), BF16),
            pltpu.VMEM((DIM, UNITS), BF16),
            pltpu.VMEM((UNITS, DIM), BF16),
            pltpu.VMEM((2, ROWS, DIM), BF16),
            pltpu.VMEM((2, DIM, ROWS), BF16),
            pltpu.VMEM((SLOTS, 3, max(SIZES), UNITS), BF16),
            pltpu.VMEM((3, ROWS, UNITS), BF16),
            pltpu.VMEM((2, 3, ROWS // 4, HY), BF16),
            pltpu.VMEM((2, 3, ROWS // 4, CY), BF16),
            pltpu.VMEM((2, 3, ROWS // 4, HY), BF16),
            pltpu.VMEM((2, 3, ROWS // 4, HY), BF16),
            pltpu.VMEM((3, ROWS // 4, HY), BF16),
            pltpu.VMEM((2, 3, ROWS // 2, CX), BF16),
            pltpu.VMEM((2, 3, ROWS // 8, HX), BF16),
            pltpu.VMEM((2, 3, ROWS // 8, CX), BF16),
            pltpu.VMEM((3, ROWS // 2, CX), BF16),
            pltpu.VMEM((3, 2, 2 * OWN, DIM), BF16),
            pltpu.VMEM((2, OWN, DIM), BF16),
            pltpu.VMEM((2, OWN, DIM), F32),
            pltpu.VMEM((3, 2, 2 * OWN, DIM), BF16),
            pltpu.VMEM((2, OWN, DIM), BF16),
            pltpu.VMEM((DIM, UNITS), BF16),
            pltpu.VMEM((DIM, UNITS), BF16),
            pltpu.VMEM((UNITS, DIM), BF16),
            pltpu.SemaphoreType.DMA((SEMS,)),
            pltpu.SemaphoreType.DMA((SEMS,)),
            pltpu.SemaphoreType.DMA((6,)),
        ],
        compiler_params=pltpu.CompilerParams(
            collective_id=0, has_side_effects=True, vmem_limit_bytes=60 * 1024 * 1024
        ),
        cost_estimate=pl.CostEstimate(flops=18 * ROWS * DIM * UNITS, bytes_accessed=16_000_000, transcendentals=0),
        name="layer",
    )(tokens[0], cotangent[0], gate_weight[0], up_weight[0], down_weight[0], frag_delta[0])
    mean_delta = (frag_delta[0].astype(F32) + other.astype(F32)) / lax.axis_size("replica")
    momentum_next = momentum_rate * outer_momentum + mean_delta
    outer_step = outer_rate * (mean_delta + momentum_rate * momentum_next)
    return (
        mixed[None], input_grad[None], gate_grad[None], up_grad[None], down_grad[None],
        outer_step, momentum_next,
    )


def solution(mesh):
    act, wide, tall = P("replica", "tensor", "dp"), P("replica", "dp", "tensor"), P("replica", "tensor", "dp")
    state = P("tensor", "dp")
    return jax.shard_map(
        shards,
        mesh=mesh,
        in_specs=(act, act, wide, wide, tall, tall, state),
        out_specs=(act, act, wide, wide, tall, state, state),
        check_vma=False,
    )
```

```python
import jax
import jax.numpy as jnp
from jax import lax
from jax.experimental import pallas as pl
from jax.experimental.pallas import tpu as pltpu
from jax.sharding import PartitionSpec as P

MESH = pl.DeviceIdType.MESH
F32 = jnp.float32
BF16 = jnp.bfloat16
momentum_rate = 0.9
outer_rate = 0.7

ROWS = 1024
OWN = 128
DIM = 512
UNITS = 1792
CHUNKS = 8
SLOTS = 3
CY = 1024
CX = UNITS - CY
HY = CY // 2
HX = CX // 2
YB = OWN // 4
XR = OWN // 2
XB = XR // 4
TILE = 256
SEMS = 342

ORDER = (
    "A0", "By0", "M0", "A1", "Bx0", "Cy0", "Bz0", "By1", "Bx1", "A2", "Cx0", "A3", "Bz1", "Cx1", "Cy1", "By2",
    "Dy0", "A4", "Dx0", "Bx2", "By3", "Bz2", "Bx3", "Dx1", "Cy2", "Bz3", "By4", "Dy1", "Ex0", "Ey0", "Cx2",
    "A5", "Bx4", "Cy3", "Cx3", "A6", "Ex1", "Bz4", "Cy4", "Fx0", "Dy2", "Fy0", "Ey1", "Dx2", "By5", "Bx5",
    "Cx4", "A7", "Dx3", "Bz5", "By6", "Fx1", "Dy3", "Bx6", "Bz6", "Fy1", "Ex2", "Cy5", "Cx5", "Dy4", "Dx4",
    "G0", "By7", "Ey2", "Ex3", "Bx7", "Cy6", "Cx6", "Bz7", "Fx2", "Dx5", "G1", "W1", "Ey3", "Ex4", "Cy7", "Dy5",
    "Fy2", "Fx3", "Cx7", "Ey4", "Dx6", "Ex5", "Dy6", "Fy3", "Fx4", "G2", "Dx7", "Fy4", "Dy7", "Ex6", "Fx5",
    "Ey5", "G3", "Ex7", "Fx6", "Ey6", "G4", "Fx7", "Fy5", "Ey7", "Fy6", "G5", "W5", "Fy7", "G6", "G7", "X0",
)


def pointwise(gate, up, hidden_grad):
    sigma = jax.nn.sigmoid(gate)
    active = gate * sigma
    hidden = active * up
    gate_slope = hidden_grad * up * sigma * (1.0 + gate * (1.0 - sigma))
    up_slope = hidden_grad * active
    return hidden.astype(BF16), gate_slope.astype(BF16), up_slope.astype(BF16)


def dot(a, b, ca=1, cb=0):
    return lax.dot_general(a, b, (((ca,), (cb,)), ((), ())), preferred_element_type=F32)


def kernel(
    tok_in, cot_in, wg_hbm, wu_hbm, wd_hbm, frag_in,
    mixed_out, ig_out, gg_out, ug_out, dg_out, frag_out,
    wg, wu, wd, tc_all, tc_t, part, h_all, ra, rb, sy, rc, e_own, xa, xb, xc, g_all, ms, ml, own, rz, rx, gg, ug, dt, dg,
    send_sem, recv_sem, local_sem,
):
    rep, d, t = lax.axis_index("replica"), lax.axis_index("dp"), lax.axis_index("tensor")
    y, xh = lax.div(d, 2), lax.rem(d, 2)
    z, xl = lax.div(t, 2), lax.rem(t, 2)
    x = 2 * xh + xl

    def at(yy, zz, xx):
        return (rep, yy * 2 + lax.div(xx, 2), zz * 2 + lax.rem(xx, 2))

    yp, ym, yo = lax.rem(y + 1, 4), lax.rem(y + 3, 4), lax.rem(y + 2, 4)
    xp, xm = lax.rem(x + 1, 4), lax.rem(x + 3, 4)
    zp, zm, zo = lax.rem(z + 1, 4), lax.rem(z + 3, 4), lax.rem(z + 2, 4)
    hp, hm = lax.div(xp, 2), lax.div(xm, 2)
    to_yp, to_ym = at(yp, z, x), at(ym, z, x)
    to_xp, to_xm = at(y, z, xp), at(y, z, xm)
    to_zp, to_zm, to_zo = at(y, zp, x), at(y, zm, x), at(y, zo, x)
    to_xl = (rep, d, 2 * z + 1 - xl)
    to_core = (1 - rep, d, t)

    count = [0]

    def remote(src, dst, target):
        k = count[0]
        count[0] += 1
        copy = pltpu.make_async_remote_copy(
            src_ref=src, dst_ref=dst, send_sem=send_sem.at[k], recv_sem=recv_sem.at[k],
            device_id=target, device_id_type=MESH,
        )
        copy.start()
        copies.append(copy)
        return copy

    copies = []
    sent = set()

    def wait_sent(copy):
        if id(copy) not in sent:
            sent.add(id(copy))
            copy.wait_send()

    loads = []
    for k, (src, dst) in enumerate(((wg_hbm, wg), (wu_hbm, wu), (wd_hbm, wd))):
        load = pltpu.make_async_copy(src, dst, local_sem.at[k])
        load.start()
        loads.append(load)

    def rows_of(start, size, step=16):
        return pl.ds(pl.multiple_of(start, step), size)

    own_rows = rows_of(t * OWN, OWN, OWN)
    mate_rows = rows_of((2 * z + 1 - xl) * OWN, OWN, OWN)
    tc_all[0, own_rows, :] = tok_in[...]
    tc_all[1, own_rows, :] = cot_in[...]

    barrier = pltpu.get_barrier_semaphore()
    peers = (to_yp, to_ym, to_xp, to_xm, to_zp, to_zm, to_zo, to_core)
    for peer in peers:
        pl.semaphore_signal(barrier, inc=1, device_id=peer, device_id_type=MESH)
    pl.semaphore_wait(barrier, len(peers))

    mate = remote(tc_all.at[:, own_rows], tc_all.at[:, own_rows], to_xl)
    gathers = {}
    frag_copy = remote(frag_in, frag_out, to_core)
    for load in loads:
        load.wait()

    live = [dict() for _ in range(CHUNKS)]

    def row0(c, side):
        zz = (z, z, zm, zp, zo, zo, zm, zp)[c]
        return (2 * zz + (1 - side if c in (1, 2, 3, 5) else side)) * OWN

    def y_rows(blk, base=0):
        return rows_of(base + blk * YB, YB)

    def x_rows(blk, base=0):
        return rows_of(base + blk * XB, XB)

    def y_own(c):
        return pl.ds(c * YB, YB)

    def x_own(c):
        return pl.ds(c * XB, XB)

    def xa_rows(c, blk):
        return x_rows(blk, c * XR)

    def stage_m(c):
        mate.wait_recv()
        for chunks, place in (((3, 2), mate_rows), ((4,), own_rows), ((5,), mate_rows), ((7, 6), own_rows)):
            for chunk in chunks:
                target = {2: to_zp, 6: to_zp, 3: to_zm, 7: to_zm, 4: to_zo, 5: to_zo}[chunk]
                gathers[chunk] = remote(tc_all.at[:, place], tc_all.at[:, place], target)

    def stage_a(c):
        s, me = c % SLOTS, live[c]
        if c in gathers:
            gathers[c].wait_recv()
        if c >= SLOTS:
            for copy in live[c - SLOTS]["part_sends"]:
                wait_sent(copy)
        rows = rows_of(row0(c, xl), OWN, OWN)

        def tile(k, carry):
            cols = pl.ds(pl.multiple_of(k * TILE, TILE), TILE)
            tok, cot = tc_all[0, rows, :], tc_all[1, rows, :]
            part[s, 0, :, cols] = dot(tok, wg[:, cols]).astype(BF16)
            part[s, 1, :, cols] = dot(tok, wu[:, cols]).astype(BF16)
            part[s, 2, :, cols] = dot(cot, wd[cols, :], 1, 1).astype(BF16)
            return carry

        lax.fori_loop(0, CY // TILE, tile, 0)
        ps = part.at[s]
        first, second = pl.ds(0, HY), pl.ds(HY, HY)
        me["s1"] = [
            remote(ps.at[:, y_rows(yo), first], ra.at[0, :, y_own(c)], to_yp),
            remote(ps.at[:, y_rows(yo), second], ra.at[1, :, y_own(c)], to_ym),
            remote(ps.at[:, y_rows(yp), second], rb.at[0, :, y_own(c), second], to_yp),
            remote(ps.at[:, y_rows(ym), first], rb.at[1, :, y_own(c), first], to_ym),
        ]
        lax.fori_loop(CY // TILE, UNITS // TILE, tile, 0)
        me["t1"] = []
        for blk in (yo, yp, ym, y):
            for k, (half, target) in enumerate(((hp, to_xp), (hm, to_xm))):
                src = ps.at[:, x_rows(blk, half * XR), pl.ds(CY, CX)]
                me["t1"].append(remote(src, xa.at[k, :, xa_rows(c, blk)], target))
        me["part_sends"] = me["s1"] + me["t1"]
        for k in range(2):
            tc_t[k, :, rows] = tc_all[k, rows, :].T

    def stage_by(c):
        s, me = c % SLOTS, live[c]
        me["s2"] = []
        for k, (blk, target) in enumerate(((yp, to_yp), (ym, to_ym))):
            rows, cols = y_rows(blk), pl.ds(k * HY, HY)
            me["s1"][k].wait_recv()
            for a in range(3):
                total = part[s, a, rows, cols].astype(F32) + ra[k, a, y_own(c), :].astype(F32)
                part[s, a, rows, cols] = total.astype(BF16)
            me["s2"].append(remote(part.at[s, :, rows, cols], rb.at[k, :, y_own(c), cols], target))
        me["part_sends"] += me["s2"]

    def add_sides(c, blk):
        rows = xa_rows(c, blk)
        for a in range(3):
            xa[0, a, rows, :] = (xa[0, a, rows, :].astype(F32) + xa[1, a, rows, :].astype(F32)).astype(BF16)

    def stage_bx(c):
        me = live[c]
        for copy in me["t1"][:2]:
            copy.wait_recv()
        add_sides(c, yo)
        rows = xa_rows(c, yo)
        me["t2"] = [
            remote(xa.at[0, :, rows, pl.ds(0, HX)], xb.at[0, :, x_own(c)], to_yp),
            remote(xa.at[0, :, rows, pl.ds(HX, HX)], xb.at[1, :, x_own(c)], to_ym),
        ]

    def stage_bz(c):
        me = live[c]
        for copy in me["t1"][2:6]:
            copy.wait_recv()
        me["t3"] = []
        for k, (blk, target) in enumerate(((yp, to_yp), (ym, to_ym))):
            add_sides(c, blk)
            cols = pl.ds((1 - k) * HX, HX)
            me["t3"].append(remote(xa.at[0, :, xa_rows(c, blk), cols], xc.at[k, :, x_own(c), cols], target))

    def stage_cy(c):
        s, me = c % SLOTS, live[c]
        for copy in me["s1"][2:] + me["s2"]:
            copy.wait_recv()
        rows, own = y_rows(y), y_own(c)
        for h in range(2):
            cols = pl.ds(h * HY, HY)
            for a in range(3):
                total = part[s, a, rows, cols].astype(F32) + rb[0, a, own, cols].astype(F32)
                sy[h, a, own, :] = (total + rb[1, a, own, cols].astype(F32)).astype(BF16)
        me["s3"] = [
            remote(sy.at[half, :, own], rc.at[k, :, own], target)
            for k, (half, target) in enumerate(((hp, to_xp), (hm, to_xm)))
        ]

    def stage_cx(c):
        me = live[c]
        for k, (blk, target) in enumerate(((yp, to_yp), (ym, to_ym))):
            rows, cols = xa_rows(c, blk), pl.ds(k * HX, HX)
            me["t2"][k].wait_recv()
            for a in range(3):
                total = xa[0, a, rows, cols].astype(F32) + xb[k, a, x_own(c), :].astype(F32)
                xa[0, a, rows, cols] = total.astype(BF16)
            me["t3"].append(remote(xa.at[0, :, rows, cols], xc.at[k, :, x_own(c), cols], target))

    def stage_dy(c):
        me, own = live[c], y_own(c)
        for copy in me["s3"]:
            copy.wait_recv()
        sums = [rc[0, a, own, :].astype(F32) + rc[1, a, own, :].astype(F32) for a in range(3)]
        for a, value in enumerate(pointwise(*sums)):
            e_own[a, own, :] = value
        place = h_all.at[:, y_rows(y, row0(c, 1 - xl)), pl.ds(pl.multiple_of(xh * HY, HY), HY)]
        me["s4"] = [remote(e_own.at[:, own], place, target) for target in (to_xp, to_xm)]

    def send_x(c, blk):
        place = h_all.at[:, x_rows(blk, row0(c, 1 - xl) + xh * XR), pl.ds(CY, CX)]
        live[c]["t6"] += [remote(g_all.at[:, xa_rows(c, blk)], place, target) for target in (to_xp, to_xm)]

    def stage_dx(c):
        me, own = live[c], x_own(c)
        for copy in me["t3"] + me["t1"][6:]:
            copy.wait_recv()
        rows = xa_rows(c, y)
        sums = []
        for a in range(3):
            total = xa[0, a, rows, :].astype(F32) + xa[1, a, rows, :].astype(F32)
            sums.append(total + (xc[0, a, own, :].astype(F32) + xc[1, a, own, :].astype(F32)))
        for a, value in enumerate(pointwise(*sums)):
            g_all[a, rows, :] = value
        place = g_all.at[:, rows]
        me["t4"] = [remote(place, place, target) for target in (to_yp, to_ym)]
        me["t6"] = []
        send_x(c, y)

    def stage_ey(c):
        me = live[c]
        for copy in me["s4"]:
            copy.wait_recv()
        place = h_all.at[:, y_rows(y, row0(c, xl)), pl.ds(0, CY)]
        me["s5"] = [remote(place, place, target) for target in (to_yp, to_ym)]

    def stage_ex(c):
        me = live[c]
        me["t5"] = []
        for k, (blk, target) in enumerate(((ym, to_yp), (yp, to_ym))):
            me["t4"][k].wait_recv()
            place = g_all.at[:, xa_rows(c, blk), pl.ds(k * HX, HX)]
            me["t5"].append(remote(place, place, target))
        for blk in (ym, yp):
            send_x(c, blk)

    def stage_fy(c):
        me = live[c]
        me["s6"] = []
        for k, (blk, target) in enumerate(((ym, to_yp), (yp, to_ym))):
            me["s5"][k].wait_recv()
            place = h_all.at[:, y_rows(blk, row0(c, xl)), pl.ds(k * HY, HY)]
            me["s6"].append(remote(place, place, target))

    def stage_fx(c):
        for copy in live[c]["t5"]:
            copy.wait_recv()
        send_x(c, yo)

    zsum = {}
    last = []
    blocks = {2: 0, 3: 1, 5: 2, 4: 3, 6: 4, 7: 5}

    def stage_g(c):
        me = live[c]
        for copy in me["s6"] + me["t6"]:
            copy.wait_recv()
        rows = rows_of(row0(c, xl), OWN, OWN)

        def keep(k, cols, value):
            if c < 2:
                own[c, k, :, cols] = value
            else:
                ms[blocks[c], k, :, cols] = value.astype(BF16)

        def mixed_tile(k, carry):
            cols = pl.ds(pl.multiple_of(k * TILE, TILE), TILE)
            keep(0, cols, dot(h_all[0, rows, :], wd[:, cols]))
            return carry

        def ig_tile(k, carry):
            cols = pl.ds(pl.multiple_of(k * TILE, TILE), TILE)
            term = dot(h_all[1, rows, :], wg[cols, :], 1, 1) + dot(h_all[2, rows, :], wu[cols, :], 1, 1)
            keep(1, cols, term)
            return carry

        zsum[c] = []
        for k, body in enumerate((mixed_tile, ig_tile)):
            lax.fori_loop(0, DIM // TILE, body, 0)
            if c >= 2:
                target = {2: to_zm, 6: to_zm, 3: to_zp, 7: to_zp, 4: to_zo, 5: to_zo}[c]
                zsum[c].append(remote(ms.at[blocks[c], k], rz.at[blocks[c], k], target))

    def z_sum(k, first):
        total = rz[first, k].astype(F32) + rz[first + 1, k].astype(F32)
        return total + rz[first + 2, k].astype(F32)

    def stage_x(c):
        for k in range(2):
            for chunk in (2, 3, 5):
                zsum[chunk][k].wait_recv()
            ml[k] = (own[1, k] + z_sum(k, 0)).astype(BF16)
            last.append(remote(ml.at[k], rx.at[k], to_xl))

    def pair(zz):
        return rows_of(2 * zz * OWN, 2 * OWN, 2 * OWN)

    def grads(places, base, out):
        def tile_of(which, a, base):
            def tile(k, carry):
                cols = pl.ds(pl.multiple_of(k * TILE, TILE), TILE)
                total = None if base is None else base[:, cols].astype(F32)
                for rows in places:
                    term = dot(tc_t[which, :, rows], h_all[a, rows, cols])
                    total = term if total is None else total + term
                out(a, cols, total.astype(BF16))
                return carry

            return tile

        for which, a, ref in ((0, 1, gg), (0, 2, ug), (1, 0, dt)):
            lax.fori_loop(0, UNITS // TILE, tile_of(which, a, None if base is None else ref), 0)
            yield a

    def kept(a, cols, value):
        {0: dt, 1: gg, 2: ug}[a][:, cols] = value

    def stored(a, cols, value):
        if a == 0:
            dg[cols, :] = value.T
        else:
            kept(a, cols, value)

    def stage_w(c):
        for _ in grads([pair(z if c == 1 else zo)], None if c == 1 else True, kept):
            pass

    stages = dict(
        A=stage_a, M=stage_m, By=stage_by, Bx=stage_bx, Bz=stage_bz, Cy=stage_cy, Cx=stage_cx, Dy=stage_dy,
        Dx=stage_dx, Ey=stage_ey, Ex=stage_ex, Fy=stage_fy, Fx=stage_fx, G=stage_g, W=stage_w, X=stage_x,
    )
    for step in ORDER:
        stages[step[:-1]](int(step[-1]))

    stores = []
    for a in grads([pair(zm), pair(zp)], True, stored):
        src, dst = {0: (dg, dg_out), 1: (gg, gg_out), 2: (ug, ug_out)}[a]
        store = pltpu.make_async_copy(src, dst, local_sem.at[3 + a])
        store.start()
        stores.append(store)

    for k, out in enumerate((mixed_out, ig_out)):
        for chunk in (4, 6, 7):
            zsum[chunk][k].wait_recv()
        total = own[0, k] + z_sum(k, 3)
        last[k].wait_recv()
        out[...] = (total + rx[k].astype(F32)).astype(BF16)
    frag_copy.wait_recv()
    for copy in copies:
        wait_sent(copy)
    for store in stores:
        store.wait()


def shards(tokens, cotangent, gate_weight, up_weight, down_weight, frag_delta, outer_momentum):
    vmem, anywhere = pl.BlockSpec(memory_space=pltpu.VMEM), pl.BlockSpec(memory_space=pl.ANY)
    side = jax.ShapeDtypeStruct((OWN, DIM), BF16)
    wide = jax.ShapeDtypeStruct((DIM, UNITS), BF16)
    tall = jax.ShapeDtypeStruct((UNITS, DIM), BF16)
    mixed, input_grad, gate_grad, up_grad, down_grad, other = pl.pallas_call(
        kernel,
        out_shape=(side, side, wide, wide, tall, tall),
        in_specs=[vmem, vmem] + [anywhere] * 4,
        out_specs=(vmem, vmem, anywhere, anywhere, anywhere, anywhere),
        scratch_shapes=[
            pltpu.VMEM((DIM, UNITS), BF16),
            pltpu.VMEM((DIM, UNITS), BF16),
            pltpu.VMEM((UNITS, DIM), BF16),
            pltpu.VMEM((2, ROWS, DIM), BF16),
            pltpu.VMEM((2, DIM, ROWS), BF16),
            pltpu.VMEM((SLOTS, 3, OWN, UNITS), BF16),
            pltpu.VMEM((3, ROWS, UNITS), BF16),
            pltpu.VMEM((2, 3, ROWS // 4, HY), BF16),
            pltpu.VMEM((2, 3, ROWS // 4, CY), BF16),
            pltpu.VMEM((2, 3, ROWS // 4, HY), BF16),
            pltpu.VMEM((2, 3, ROWS // 4, HY), BF16),
            pltpu.VMEM((3, ROWS // 4, HY), BF16),
            pltpu.VMEM((2, 3, ROWS // 2, CX), BF16),
            pltpu.VMEM((2, 3, ROWS // 8, HX), BF16),
            pltpu.VMEM((2, 3, ROWS // 8, CX), BF16),
            pltpu.VMEM((3, ROWS // 2, CX), BF16),
            pltpu.VMEM((6, 2, OWN, DIM), BF16),
            pltpu.VMEM((2, OWN, DIM), BF16),
            pltpu.VMEM((2, 2, OWN, DIM), F32),
            pltpu.VMEM((6, 2, OWN, DIM), BF16),
            pltpu.VMEM((2, OWN, DIM), BF16),
            pltpu.VMEM((DIM, UNITS), BF16),
            pltpu.VMEM((DIM, UNITS), BF16),
            pltpu.VMEM((DIM, UNITS), BF16),
            pltpu.VMEM((UNITS, DIM), BF16),
            pltpu.SemaphoreType.DMA((SEMS,)),
            pltpu.SemaphoreType.DMA((SEMS,)),
            pltpu.SemaphoreType.DMA((6,)),
        ],
        compiler_params=pltpu.CompilerParams(
            collective_id=0, has_side_effects=True, vmem_limit_bytes=56 * 1024 * 1024
        ),
        cost_estimate=pl.CostEstimate(flops=18 * ROWS * DIM * UNITS, bytes_accessed=16_000_000, transcendentals=0),
        name="layer",
    )(tokens[0], cotangent[0], gate_weight[0], up_weight[0], down_weight[0], frag_delta[0])
    mean_delta = (frag_delta[0].astype(F32) + other.astype(F32)) / lax.axis_size("replica")
    momentum_next = momentum_rate * outer_momentum + mean_delta
    outer_step = outer_rate * (mean_delta + momentum_rate * momentum_next)
    return (
        mixed[None], input_grad[None], gate_grad[None], up_grad[None], down_grad[None],
        outer_step, momentum_next,
    )


def solution(mesh):
    act, wide, tall = P("replica", "tensor", "dp"), P("replica", "dp", "tensor"), P("replica", "tensor", "dp")
    state = P("tensor", "dp")
    return jax.shard_map(
        shards,
        mesh=mesh,
        in_specs=(act, act, wide, wide, tall, tall, state),
        out_specs=(act, act, wide, wide, tall, state, state),
        check_vma=False,
    )
```

```python
import jax
import jax.numpy as jnp
from jax import lax
from jax.experimental import pallas as pl
from jax.experimental.pallas import tpu as pltpu
from jax.sharding import PartitionSpec as P

MESH = pl.DeviceIdType.MESH
F32 = jnp.float32
BF16 = jnp.bfloat16
momentum_rate = 0.9
outer_rate = 0.7

ROWS = 1024
OWN = 128
DIM = 512
UNITS = 1792
CHUNKS = 8
SLOTS = 4
CY = 1024
CX = UNITS - CY
HY = CY // 2
HX = CX // 2
YB = OWN // 4
XR = OWN // 2
XB = XR // 4
TILE = 256
SEMS = 342

ORDER = (
    "A0", "By0", "M0", "A1", "Bx0", "Bz0", "Cy0", "A2", "By1", "Bx1", "A3", "Cx0", "Bz1", "A4", "Dy0", "By2",
    "Bx2", "Cy1", "Cx1", "A5", "Bz2", "By3", "Bx3", "Dx0", "Bz3", "By4", "Bx4", "Cy2", "Cx2", "Bz4", "A6",
    "Dx1", "By5", "Ey0", "Dy1", "Bx5", "Cy3", "Cx3", "A7", "Bz5", "Ex0", "Cy4", "Cx4", "Dx2", "Dy2", "Bx6",
    "By6", "Bz6", "Ex1", "Cy5", "Ey1", "Fy0", "Dy3", "Cx5", "Dx3", "Bx7", "By7", "Bz7", "Fx0", "Dx4", "Ex2",
    "Cx6", "Dy4", "Cy6", "Fx1", "Ey2", "Fy1", "Dy5", "Dx5", "Ex3", "Ey3", "Cx7", "Cy7", "G0", "Ex4", "Fx2",
    "Dx6", "Ey4", "Fy2", "Dy6", "G1", "W1", "Ex5", "Ey5", "Fx3", "Fy3", "Dx7", "Fx4", "Dy7", "Ex6", "Fy4", "G2",
    "Fx5", "Ey6", "Fy5", "G3", "Ex7", "Fx6", "G4", "Ey7", "Fy6", "G5", "W5", "Fx7", "Fy7", "G6", "G7", "X0",
)


def pointwise(gate, up, hidden_grad):
    sigma = jax.nn.sigmoid(gate)
    active = gate * sigma
    hidden = active * up
    gate_slope = hidden_grad * up * sigma * (1.0 + gate * (1.0 - sigma))
    up_slope = hidden_grad * active
    return hidden.astype(BF16), gate_slope.astype(BF16), up_slope.astype(BF16)


def dot(a, b, ca=1, cb=0):
    return lax.dot_general(a, b, (((ca,), (cb,)), ((), ())), preferred_element_type=F32)


def kernel(
    tok_in, cot_in, wg_hbm, wu_hbm, wd_hbm, frag_in,
    mixed_out, ig_out, gg_out, ug_out, dg_out, frag_out,
    wg, wu, wd, tc_all, tc_t, part, h_all, ra, rb, sy, rc, e_own, xa, xb, xc, g_all, ms, ml, own, rz, rx, gg, ug, dt, dg,
    send_sem, recv_sem, local_sem,
):
    rep, d, t = lax.axis_index("replica"), lax.axis_index("dp"), lax.axis_index("tensor")
    y, xh = lax.div(d, 2), lax.rem(d, 2)
    z, xl = lax.div(t, 2), lax.rem(t, 2)
    x = 2 * xh + xl

    def at(yy, zz, xx):
        return (rep, yy * 2 + lax.div(xx, 2), zz * 2 + lax.rem(xx, 2))

    yp, ym, yo = lax.rem(y + 1, 4), lax.rem(y + 3, 4), lax.rem(y + 2, 4)
    xp, xm = lax.rem(x + 1, 4), lax.rem(x + 3, 4)
    zp, zm, zo = lax.rem(z + 1, 4), lax.rem(z + 3, 4), lax.rem(z + 2, 4)
    hp, hm = lax.div(xp, 2), lax.div(xm, 2)
    to_yp, to_ym = at(yp, z, x), at(ym, z, x)
    to_xp, to_xm = at(y, z, xp), at(y, z, xm)
    to_zp, to_zm, to_zo = at(y, zp, x), at(y, zm, x), at(y, zo, x)
    to_xl = (rep, d, 2 * z + 1 - xl)
    to_core = (1 - rep, d, t)

    count = [0]

    def remote(src, dst, target):
        k = count[0]
        count[0] += 1
        copy = pltpu.make_async_remote_copy(
            src_ref=src, dst_ref=dst, send_sem=send_sem.at[k], recv_sem=recv_sem.at[k],
            device_id=target, device_id_type=MESH,
        )
        copy.start()
        copies.append(copy)
        return copy

    copies = []
    sent = set()

    def wait_sent(copy):
        if id(copy) not in sent:
            sent.add(id(copy))
            copy.wait_send()

    loads = []
    for k, (src, dst) in enumerate(((wg_hbm, wg), (wu_hbm, wu), (wd_hbm, wd))):
        load = pltpu.make_async_copy(src, dst, local_sem.at[k])
        load.start()
        loads.append(load)

    def rows_of(start, size, step=16):
        return pl.ds(pl.multiple_of(start, step), size)

    own_rows = rows_of(t * OWN, OWN, OWN)
    mate_rows = rows_of((2 * z + 1 - xl) * OWN, OWN, OWN)
    tc_all[0, own_rows, :] = tok_in[...]
    tc_all[1, own_rows, :] = cot_in[...]

    barrier = pltpu.get_barrier_semaphore()
    peers = (to_yp, to_ym, to_xp, to_xm, to_zp, to_zm, to_zo, to_core)
    for peer in peers:
        pl.semaphore_signal(barrier, inc=1, device_id=peer, device_id_type=MESH)
    pl.semaphore_wait(barrier, len(peers))

    mate = remote(tc_all.at[:, own_rows], tc_all.at[:, own_rows], to_xl)
    gathers = {}
    frag_copy = remote(frag_in, frag_out, to_core)
    for load in loads:
        load.wait()

    live = [dict() for _ in range(CHUNKS)]

    def row0(c, side):
        zz = (z, z, zm, zp, zo, zo, zm, zp)[c]
        return (2 * zz + (1 - side if c in (1, 2, 3, 5) else side)) * OWN

    def y_rows(blk, base=0):
        return rows_of(base + blk * YB, YB)

    def x_rows(blk, base=0):
        return rows_of(base + blk * XB, XB)

    def y_own(c):
        return pl.ds(c * YB, YB)

    def x_own(c):
        return pl.ds(c * XB, XB)

    def xa_rows(c, blk):
        return x_rows(blk, c * XR)

    def stage_m(c):
        mate.wait_recv()
        for chunks, place in (((3, 2), mate_rows), ((4,), own_rows), ((5,), mate_rows), ((7, 6), own_rows)):
            for chunk in chunks:
                target = {2: to_zp, 6: to_zp, 3: to_zm, 7: to_zm, 4: to_zo, 5: to_zo}[chunk]
                gathers[chunk] = remote(tc_all.at[:, place], tc_all.at[:, place], target)

    def stage_a(c):
        s, me = c % SLOTS, live[c]
        if c in gathers:
            gathers[c].wait_recv()
        if c >= SLOTS:
            for copy in live[c - SLOTS]["part_sends"]:
                wait_sent(copy)
        rows = rows_of(row0(c, xl), OWN, OWN)

        def tile(k, carry):
            cols = pl.ds(pl.multiple_of(k * TILE, TILE), TILE)
            tok, cot = tc_all[0, rows, :], tc_all[1, rows, :]
            part[s, 0, :, cols] = dot(tok, wg[:, cols]).astype(BF16)
            part[s, 1, :, cols] = dot(tok, wu[:, cols]).astype(BF16)
            part[s, 2, :, cols] = dot(cot, wd[cols, :], 1, 1).astype(BF16)
            return carry

        lax.fori_loop(0, CY // TILE, tile, 0)
        ps = part.at[s]
        first, second = pl.ds(0, HY), pl.ds(HY, HY)
        me["s1"] = [
            remote(ps.at[:, y_rows(yo), first], ra.at[0, :, y_own(c)], to_yp),
            remote(ps.at[:, y_rows(yo), second], ra.at[1, :, y_own(c)], to_ym),
            remote(ps.at[:, y_rows(yp), second], rb.at[0, :, y_own(c), second], to_yp),
            remote(ps.at[:, y_rows(ym), first], rb.at[1, :, y_own(c), first], to_ym),
        ]
        lax.fori_loop(CY // TILE, UNITS // TILE, tile, 0)
        me["t1"] = []
        for blk in (yo, yp, ym, y):
            for k, (half, target) in enumerate(((hp, to_xp), (hm, to_xm))):
                src = ps.at[:, x_rows(blk, half * XR), pl.ds(CY, CX)]
                me["t1"].append(remote(src, xa.at[k, :, xa_rows(c, blk)], target))
        me["part_sends"] = me["s1"] + me["t1"]
        for k in range(2):
            tc_t[k, :, rows] = tc_all[k, rows, :].T

    def stage_by(c):
        s, me = c % SLOTS, live[c]
        me["s2"] = []
        for k, (blk, target) in enumerate(((yp, to_yp), (ym, to_ym))):
            rows, cols = y_rows(blk), pl.ds(k * HY, HY)
            me["s1"][k].wait_recv()
            for a in range(3):
                total = part[s, a, rows, cols].astype(F32) + ra[k, a, y_own(c), :].astype(F32)
                part[s, a, rows, cols] = total.astype(BF16)
            me["s2"].append(remote(part.at[s, :, rows, cols], rb.at[k, :, y_own(c), cols], target))
        me["part_sends"] += me["s2"]

    def add_sides(c, blk):
        rows = xa_rows(c, blk)
        for a in range(3):
            xa[0, a, rows, :] = (xa[0, a, rows, :].astype(F32) + xa[1, a, rows, :].astype(F32)).astype(BF16)

    def stage_bx(c):
        me = live[c]
        for copy in me["t1"][:2]:
            copy.wait_recv()
        add_sides(c, yo)
        rows = xa_rows(c, yo)
        me["t2"] = [
            remote(xa.at[0, :, rows, pl.ds(0, HX)], xb.at[0, :, x_own(c)], to_yp),
            remote(xa.at[0, :, rows, pl.ds(HX, HX)], xb.at[1, :, x_own(c)], to_ym),
        ]

    def stage_bz(c):
        me = live[c]
        for copy in me["t1"][2:6]:
            copy.wait_recv()
        me["t3"] = []
        for k, (blk, target) in enumerate(((yp, to_yp), (ym, to_ym))):
            add_sides(c, blk)
            cols = pl.ds((1 - k) * HX, HX)
            me["t3"].append(remote(xa.at[0, :, xa_rows(c, blk), cols], xc.at[k, :, x_own(c), cols], target))

    def stage_cy(c):
        s, me = c % SLOTS, live[c]
        for copy in me["s1"][2:] + me["s2"]:
            copy.wait_recv()
        rows, own = y_rows(y), y_own(c)
        for h in range(2):
            cols = pl.ds(h * HY, HY)
            for a in range(3):
                total = part[s, a, rows, cols].astype(F32) + rb[0, a, own, cols].astype(F32)
                sy[h, a, own, :] = (total + rb[1, a, own, cols].astype(F32)).astype(BF16)
        me["s3"] = [
            remote(sy.at[half, :, own], rc.at[k, :, own], target)
            for k, (half, target) in enumerate(((hp, to_xp), (hm, to_xm)))
        ]

    def stage_cx(c):
        me = live[c]
        for k, (blk, target) in enumerate(((yp, to_yp), (ym, to_ym))):
            rows, cols = xa_rows(c, blk), pl.ds(k * HX, HX)
            me["t2"][k].wait_recv()
            for a in range(3):
                total = xa[0, a, rows, cols].astype(F32) + xb[k, a, x_own(c), :].astype(F32)
                xa[0, a, rows, cols] = total.astype(BF16)
            me["t3"].append(remote(xa.at[0, :, rows, cols], xc.at[k, :, x_own(c), cols], target))

    def stage_dy(c):
        me, own = live[c], y_own(c)
        for copy in me["s3"]:
            copy.wait_recv()
        sums = [rc[0, a, own, :].astype(F32) + rc[1, a, own, :].astype(F32) for a in range(3)]
        for a, value in enumerate(pointwise(*sums)):
            e_own[a, own, :] = value
        place = h_all.at[:, y_rows(y, row0(c, 1 - xl)), pl.ds(pl.multiple_of(xh * HY, HY), HY)]
        me["s4"] = [remote(e_own.at[:, own], place, target) for target in (to_xp, to_xm)]

    def send_x(c, blk):
        place = h_all.at[:, x_rows(blk, row0(c, 1 - xl) + xh * XR), pl.ds(CY, CX)]
        live[c]["t6"] += [remote(g_all.at[:, xa_rows(c, blk)], place, target) for target in (to_xp, to_xm)]

    def stage_dx(c):
        me, own = live[c], x_own(c)
        for copy in me["t3"] + me["t1"][6:]:
            copy.wait_recv()
        rows = xa_rows(c, y)
        sums = []
        for a in range(3):
            total = xa[0, a, rows, :].astype(F32) + xa[1, a, rows, :].astype(F32)
            sums.append(total + (xc[0, a, own, :].astype(F32) + xc[1, a, own, :].astype(F32)))
        for a, value in enumerate(pointwise(*sums)):
            g_all[a, rows, :] = value
        place = g_all.at[:, rows]
        me["t4"] = [remote(place, place, target) for target in (to_yp, to_ym)]
        me["t6"] = []
        send_x(c, y)

    def stage_ey(c):
        me = live[c]
        for copy in me["s4"]:
            copy.wait_recv()
        place = h_all.at[:, y_rows(y, row0(c, xl)), pl.ds(0, CY)]
        me["s5"] = [remote(place, place, target) for target in (to_yp, to_ym)]

    def stage_ex(c):
        me = live[c]
        me["t5"] = []
        for k, (blk, target) in enumerate(((ym, to_yp), (yp, to_ym))):
            me["t4"][k].wait_recv()
            place = g_all.at[:, xa_rows(c, blk), pl.ds(k * HX, HX)]
            me["t5"].append(remote(place, place, target))
        for blk in (ym, yp):
            send_x(c, blk)

    def stage_fy(c):
        me = live[c]
        me["s6"] = []
        for k, (blk, target) in enumerate(((ym, to_yp), (yp, to_ym))):
            me["s5"][k].wait_recv()
            place = h_all.at[:, y_rows(blk, row0(c, xl)), pl.ds(k * HY, HY)]
            me["s6"].append(remote(place, place, target))

    def stage_fx(c):
        for copy in live[c]["t5"]:
            copy.wait_recv()
        send_x(c, yo)

    zsum = {}
    last = []
    blocks = {2: 0, 3: 1, 5: 2, 4: 3, 6: 4, 7: 5}

    def stage_g(c):
        me = live[c]
        for copy in me["s6"] + me["t6"]:
            copy.wait_recv()
        rows = rows_of(row0(c, xl), OWN, OWN)

        def keep(k, cols, value):
            if c < 2:
                own[c, k, :, cols] = value
            else:
                ms[blocks[c], k, :, cols] = value.astype(BF16)

        def mixed_tile(k, carry):
            cols = pl.ds(pl.multiple_of(k * TILE, TILE), TILE)
            keep(0, cols, dot(h_all[0, rows, :], wd[:, cols]))
            return carry

        def ig_tile(k, carry):
            cols = pl.ds(pl.multiple_of(k * TILE, TILE), TILE)
            term = dot(h_all[1, rows, :], wg[cols, :], 1, 1) + dot(h_all[2, rows, :], wu[cols, :], 1, 1)
            keep(1, cols, term)
            return carry

        zsum[c] = []
        for k, body in enumerate((mixed_tile, ig_tile)):
            lax.fori_loop(0, DIM // TILE, body, 0)
            if c >= 2:
                target = {2: to_zm, 6: to_zm, 3: to_zp, 7: to_zp, 4: to_zo, 5: to_zo}[c]
                zsum[c].append(remote(ms.at[blocks[c], k], rz.at[blocks[c], k], target))

    def z_sum(k, first):
        total = rz[first, k].astype(F32) + rz[first + 1, k].astype(F32)
        return total + rz[first + 2, k].astype(F32)

    def stage_x(c):
        for k in range(2):
            for chunk in (2, 3, 5):
                zsum[chunk][k].wait_recv()
            ml[k] = (own[1, k] + z_sum(k, 0)).astype(BF16)
            last.append(remote(ml.at[k], rx.at[k], to_xl))

    def pair(zz):
        return rows_of(2 * zz * OWN, 2 * OWN, 2 * OWN)

    def grads(places, base, out):
        def tile_of(which, a, base):
            def tile(k, carry):
                cols = pl.ds(pl.multiple_of(k * TILE, TILE), TILE)
                total = None if base is None else base[:, cols].astype(F32)
                for rows in places:
                    term = dot(tc_t[which, :, rows], h_all[a, rows, cols])
                    total = term if total is None else total + term
                out(a, cols, total.astype(BF16))
                return carry

            return tile

        for which, a, ref in ((0, 1, gg), (0, 2, ug), (1, 0, dt)):
            lax.fori_loop(0, UNITS // TILE, tile_of(which, a, None if base is None else ref), 0)
            yield a

    def kept(a, cols, value):
        {0: dt, 1: gg, 2: ug}[a][:, cols] = value

    def stored(a, cols, value):
        if a == 0:
            dg[cols, :] = value.T
        else:
            kept(a, cols, value)

    def stage_w(c):
        for _ in grads([pair(z if c == 1 else zo)], None if c == 1 else True, kept):
            pass

    stages = dict(
        A=stage_a, M=stage_m, By=stage_by, Bx=stage_bx, Bz=stage_bz, Cy=stage_cy, Cx=stage_cx, Dy=stage_dy,
        Dx=stage_dx, Ey=stage_ey, Ex=stage_ex, Fy=stage_fy, Fx=stage_fx, G=stage_g, W=stage_w, X=stage_x,
    )
    for step in ORDER:
        stages[step[:-1]](int(step[-1]))

    stores = []
    for a in grads([pair(zm), pair(zp)], True, stored):
        src, dst = {0: (dg, dg_out), 1: (gg, gg_out), 2: (ug, ug_out)}[a]
        store = pltpu.make_async_copy(src, dst, local_sem.at[3 + a])
        store.start()
        stores.append(store)

    for k, out in enumerate((mixed_out, ig_out)):
        for chunk in (4, 6, 7):
            zsum[chunk][k].wait_recv()
        total = own[0, k] + z_sum(k, 3)
        last[k].wait_recv()
        out[...] = (total + rx[k].astype(F32)).astype(BF16)
    frag_copy.wait_recv()
    for copy in copies:
        wait_sent(copy)
    for store in stores:
        store.wait()


def shards(tokens, cotangent, gate_weight, up_weight, down_weight, frag_delta, outer_momentum):
    vmem, anywhere = pl.BlockSpec(memory_space=pltpu.VMEM), pl.BlockSpec(memory_space=pl.ANY)
    side = jax.ShapeDtypeStruct((OWN, DIM), BF16)
    wide = jax.ShapeDtypeStruct((DIM, UNITS), BF16)
    tall = jax.ShapeDtypeStruct((UNITS, DIM), BF16)
    mixed, input_grad, gate_grad, up_grad, down_grad, other = pl.pallas_call(
        kernel,
        out_shape=(side, side, wide, wide, tall, tall),
        in_specs=[vmem, vmem] + [anywhere] * 4,
        out_specs=(vmem, vmem, anywhere, anywhere, anywhere, anywhere),
        scratch_shapes=[
            pltpu.VMEM((DIM, UNITS), BF16),
            pltpu.VMEM((DIM, UNITS), BF16),
            pltpu.VMEM((UNITS, DIM), BF16),
            pltpu.VMEM((2, ROWS, DIM), BF16),
            pltpu.VMEM((2, DIM, ROWS), BF16),
            pltpu.VMEM((SLOTS, 3, OWN, UNITS), BF16),
            pltpu.VMEM((3, ROWS, UNITS), BF16),
            pltpu.VMEM((2, 3, ROWS // 4, HY), BF16),
            pltpu.VMEM((2, 3, ROWS // 4, CY), BF16),
            pltpu.VMEM((2, 3, ROWS // 4, HY), BF16),
            pltpu.VMEM((2, 3, ROWS // 4, HY), BF16),
            pltpu.VMEM((3, ROWS // 4, HY), BF16),
            pltpu.VMEM((2, 3, ROWS // 2, CX), BF16),
            pltpu.VMEM((2, 3, ROWS // 8, HX), BF16),
            pltpu.VMEM((2, 3, ROWS // 8, CX), BF16),
            pltpu.VMEM((3, ROWS // 2, CX), BF16),
            pltpu.VMEM((6, 2, OWN, DIM), BF16),
            pltpu.VMEM((2, OWN, DIM), BF16),
            pltpu.VMEM((2, 2, OWN, DIM), F32),
            pltpu.VMEM((6, 2, OWN, DIM), BF16),
            pltpu.VMEM((2, OWN, DIM), BF16),
            pltpu.VMEM((DIM, UNITS), BF16),
            pltpu.VMEM((DIM, UNITS), BF16),
            pltpu.VMEM((DIM, UNITS), BF16),
            pltpu.VMEM((UNITS, DIM), BF16),
            pltpu.SemaphoreType.DMA((SEMS,)),
            pltpu.SemaphoreType.DMA((SEMS,)),
            pltpu.SemaphoreType.DMA((6,)),
        ],
        compiler_params=pltpu.CompilerParams(
            collective_id=0, has_side_effects=True, vmem_limit_bytes=56 * 1024 * 1024
        ),
        cost_estimate=pl.CostEstimate(flops=18 * ROWS * DIM * UNITS, bytes_accessed=16_000_000, transcendentals=0),
        name="layer",
    )(tokens[0], cotangent[0], gate_weight[0], up_weight[0], down_weight[0], frag_delta[0])
    mean_delta = (frag_delta[0].astype(F32) + other.astype(F32)) / lax.axis_size("replica")
    momentum_next = momentum_rate * outer_momentum + mean_delta
    outer_step = outer_rate * (mean_delta + momentum_rate * momentum_next)
    return (
        mixed[None], input_grad[None], gate_grad[None], up_grad[None], down_grad[None],
        outer_step, momentum_next,
    )


def solution(mesh):
    act, wide, tall = P("replica", "tensor", "dp"), P("replica", "dp", "tensor"), P("replica", "tensor", "dp")
    state = P("tensor", "dp")
    return jax.shard_map(
        shards,
        mesh=mesh,
        in_specs=(act, act, wide, wide, tall, tall, state),
        out_specs=(act, act, wide, wide, tall, state, state),
        check_vma=False,
    )
```
